32 devices in a mesh: dp: 8 (over z, y), tensor: 4 (over x, core).
Axes of the slice: x: 2, y: 2, z: 4, core: 2. Of those that a mesh axis runs over, the one named last changes fastest.
Arguments:
- gate_pre: bfloat16 [32, 64, 28672], P('dp', None, 'tensor'), may hold values from -6 to 6
- up_pre: bfloat16 [32, 64, 28672], P('dp', None, 'tensor'), may hold values from -6 to 6
- out_grad: bfloat16 [32, 64, 8192], P('dp', None, 'tensor'), may hold values from -60 to 60
- lengths: int32 [32], P('dp'), may hold values from 1 to 64, 1280 in all
- proj_hidden: bfloat16 [28672, 64], P('tensor'), may hold values from -0.03125 to 0.03125
- proj_out: bfloat16 [8192, 64], P('tensor'), may hold values from -0.0625 to 0.0625
- query_grads: float32 [64, 4096], P('dp'), may hold values from -6 to 6
Outputs:
- scores: float32 [32, 64], P('dp')
The draws below stay inside these ranges and needn't reach their ends.
Inputs may be any that keep to these rules, and one draw needn't show every extreme that they name: `lengths`: each example has 1 to 64 live tokens, and some example has exactly 64.
All inputs are finite; a program needn't handle non-finite values. No bound on the sum of `lengths` on one device may be relied on, other than what follows from the above.
Results may differ from the reference program's by a relative error of at most 0.003.
Values sent between devices are 32-bit elements; how exact they have to be, the bound alone decides.
A program may use at most 64 MiB of HBM per device.

```python
import math
import jax
import jax.numpy as jnp
import numpy as np
from jax import lax

D = 8192
FF = 28672
SEQ = 64
RANK = 64
EXAMPLES = 32
QUERIES = 64


def draw_out_grad(key, part):
    key_base = jax.random.fold_in(key, 11)
    key_scale = jax.random.fold_in(key, 23)
    position = jnp.arange(EXAMPLES, dtype=jnp.float32) / max(EXAMPLES - 1, 1)
    rising = jnp.exp(math.log(3.0) * position)
    base = jnp.clip(jax.random.normal(key_base, (EXAMPLES, SEQ, D), jnp.float32), -5.0, 5.0)
    factor = jax.random.uniform(key_scale, (EXAMPLES,), jnp.float32, 1.0, 2.0)
    scale = rising * factor
    return (base * scale[:, None, None]).astype(jnp.bfloat16)


def levels(rng, shape, pieces, low, top_value):
    loudness = 1.0
    for dim, blocks in pieces:
        draws = jax.random.uniform(jax.random.fold_in(jax.random.fold_in(rng, 6), dim), (blocks,), jnp.float32, low / len(pieces), top_value / len(pieces))
        loudness = loudness * jnp.repeat(jnp.exp(draws), shape[dim] // blocks).reshape((-1,) + (1,) * (len(shape) - 1 - dim))
    return loudness


def profile(number_of, total, bound, skew):
    portions = [(1 << 20) // math.isqrt(grade ** skew) + 1 for grade in range(2, number_of + 1)]
    rest, holding = total - bound - (number_of - 1), [1] * (number_of - 1)
    while rest > 0:
        candidates = [i for i in range(number_of - 1) if holding[i] < bound]
        mass, remaining = sum([portions[i] for i in candidates]), rest
        for i in candidates:
            more = min(bound - holding[i], max(1, remaining * portions[i] // mass), rest)
            holding[i] = holding[i] + more
            rest = rest - more
    return np.array([bound] + holding)


def uneven_parts(stream_key, amount, total, most, skew):
    if amount == 2:
        one = jax.random.randint(stream_key, (), max(1, total - most), min(most, total - 1) + 1)
        return jnp.stack([one, total - one])
    sizes = jnp.asarray(profile(amount, total, most, skew), jnp.int32)
    twos = (amount - 1) // 2
    source_of, receiver = sizes[1:1 + 2 * twos:2], sizes[2:2 + 2 * twos:2]
    room = jnp.minimum(source_of - 1, most - receiver)
    shifted = jax.random.randint(jax.random.fold_in(stream_key, 1), (twos,), 0, 1 << 20) % (room + 1)
    sizes = sizes.at[1:1 + 2 * twos:2].set(source_of - shifted).at[2:2 + 2 * twos:2].set(receiver + shifted)
    return sizes[jax.random.permutation(jax.random.fold_in(stream_key, 2), amount)]


def scatter_about(own_key, shape, scale, most, shards=(), kind=jnp.bfloat16):
    factor_of = levels(own_key, shape, shards, -0.22, 0.18) if shards else 1.0
    result = jax.random.normal(own_key, shape, jnp.float32) * scale * factor_of
    return jnp.minimum(jnp.maximum(result, -most), most).astype(kind)


def setup_inputs(seed: int = 0) -> dict:
    key_list = jax.random.split(jax.random.key(seed), 8)
    return {
        "gate_pre": scatter_about(key_list[0], (EXAMPLES, SEQ, FF), 1.0, 6.0, ((0, 8), (2, 4))),
        "up_pre": scatter_about(key_list[1], (EXAMPLES, SEQ, FF), 1.0, 6.0, ((0, 8), (2, 4))),
        "out_grad": draw_out_grad(jax.random.fold_in(key_list[7], 71), 0),
        "lengths": uneven_parts(key_list[3], EXAMPLES, EXAMPLES * SEQ * 5 // 8, SEQ, 1).astype(jnp.int32),
        "proj_hidden": scatter_about(key_list[4], (FF, RANK), FF ** -0.5, 0.03125, ((0, 4),)),
        "proj_out": scatter_about(key_list[5], (D, RANK), D ** -0.5, 0.0625, ((0, 4),)),
        "query_grads": scatter_about(key_list[6], (QUERIES, RANK * RANK), 1.0, 6.0, ((0, 8),), jnp.float32),
    }


def reference(gate_pre, up_pre, out_grad, lengths, proj_hidden, proj_out, query_grads):
    def one_example(items):
        gate_rows, up_rows, grad_rows, length = items
        hidden = (jax.nn.silu(gate_rows.astype(jnp.float32)) * up_rows.astype(jnp.float32)).astype(jnp.bfloat16)
        in_proj = jnp.dot(hidden, proj_hidden, preferred_element_type=jnp.float32)
        live = (jnp.arange(SEQ, dtype=jnp.int32) < length).astype(jnp.float32)
        in_proj = in_proj * live[:, None]
        out_proj = jnp.dot(grad_rows, proj_out, preferred_element_type=jnp.float32)
        outer = jnp.dot(in_proj.T, out_proj, precision=lax.Precision.HIGHEST, preferred_element_type=jnp.float32)
        return outer.reshape(RANK * RANK)

    train_grads = lax.map(one_example, (gate_pre, up_pre, out_grad, lengths))
    moment = jnp.mean(train_grads * train_grads, axis=0)
    precond = 1.0 / (moment + 0.1 * jnp.mean(moment))
    weighted = train_grads * precond[None, :]
    scores = jnp.dot(weighted, query_grads.T, precision=lax.Precision.HIGHEST, preferred_element_type=jnp.float32)
    return scores / RANK
```

```python
import functools

import jax
import jax.numpy as jnp
from jax import lax
from jax.experimental import pallas as pl
from jax.experimental.pallas import tpu as pltpu
from jax.sharding import PartitionSpec as P

MESH = pl.DeviceIdType.MESH
LANES = 128
DAMPING = 0.1


def contract_last(a, b, precision=None):
    return lax.dot_general(
        a, b, (((1,), (1,)), ((), ())), precision=precision, preferred_element_type=jnp.float32
    )


def pieces(size, most):
    count = -(-size // most)
    while size % (count * LANES):
        count += 1
    return count, size // count


def kernel(
    ndp,
    nt,
    length_ref,
    gate_hbm,
    up_hbm,
    grad_hbm,
    wh_hbm,
    wo_hbm,
    query_hbm,
    out_ref,
    gate,
    up,
    grad,
    wh,
    wo,
    queries,
    send1,
    recv1,
    tg_ref,
    send2,
    recv2,
    send3,
    recv3,
    gate_sem,
    up_sem,
    grad_sem,
    wh_sem,
    wo_sem,
    query_sem,
    query_send,
    query_recv,
    send1_sem,
    recv1_sem,
    send2_sem,
    recv2_sem,
    send3_sem,
    recv3_sem,
):
    seq = gate.shape[1]
    rank = wh.shape[0]
    halves, half = gate_sem.shape[1], gate.shape[2] // gate_sem.shape[1]
    feats = grad.shape[2]
    slices = rank * rank // LANES
    group = slices // nt
    ndev = ndp * nt
    nq = queries.shape[0] * queries.shape[1]
    pack = max(1, LANES // nq)
    per_row = nt // pack

    dp = lax.axis_index("dp")
    t = lax.axis_index("tensor")
    me = dp * nt + t

    def slice_of(d, x):
        return lax.rem(d, group) * nt + x

    def slot_of(d, x):
        g, local = d // group, lax.rem(d, group)
        return g * slices + lax.rem(x, pack) * (slices // pack) + local * per_row + x // pack

    def peer(i):
        p = lax.rem(me + i, ndev)
        return p // nt, lax.rem(p, nt)

    def example(s):
        return lax.rem(t + 1 + s, nt)

    barrier = pltpu.get_barrier_semaphore()

    def greet(i, c):
        pl.semaphore_signal(barrier, inc=1, device_id=peer(i), device_id_type=MESH)
        return c

    def gate_copy(e, h):
        cols = pl.ds(h * half, half)
        return pltpu.make_async_copy(
            gate_hbm.at[e, :, cols], gate.at[e, :, cols], gate_sem.at[e, h]
        )

    def up_copy(e, h):
        cols = pl.ds(h * half, half)
        return pltpu.make_async_copy(up_hbm.at[e, :, cols], up.at[e, :, cols], up_sem.at[e, h])

    def grad_copy(e):
        return pltpu.make_async_copy(grad_hbm.at[e], grad.at[e], grad_sem.at[e])

    def wh_copy(h):
        cols = pl.ds(h * half, half)
        return pltpu.make_async_copy(wh_hbm.at[:, cols], wh.at[:, cols], wh_sem.at[h])

    def query_cols(d):
        return pl.ds(pl.multiple_of(slice_of(d, t) * LANES, LANES), LANES)

    wo_copy = pltpu.make_async_copy(wo_hbm, wo, wo_sem)
    own_query = pltpu.make_async_copy(query_hbm.at[:, query_cols(dp)], queries.at[dp], query_sem)

    wo_copy.start()
    for s in range(nt):
        e = example(s)
        grad_copy(e).start()
        for h in range(halves):
            if s == 0:
                wh_copy(h).start()
            gate_copy(e, h).start()
            up_copy(e, h).start()
    own_query.start()
    lax.fori_loop(1, ndev, greet, 0)
    wo_copy.wait()

    def partial_of(s):
        e = example(s)
        grad_copy(e).wait()
        out_part = contract_last(grad[e], wo[...])
        in_part = jnp.zeros((seq, rank), jnp.float32)
        for h in range(halves):
            if s == 0:
                wh_copy(h).wait()
            gate_copy(e, h).wait()
            up_copy(e, h).wait()
            count, width = pieces(half, 512)
            for c in range(count):
                cols = pl.ds(h * half + c * width, width)
                a = gate[e, :, cols].astype(jnp.float32) * 0.5
                u = up[e, :, cols].astype(jnp.float32)
                hidden = (u * (a + a * jnp.tanh(a))).astype(jnp.bfloat16)
                in_part = in_part + contract_last(hidden, wh[:, cols])
        return jnp.concatenate([in_part, out_part], axis=1)

    def reduce_copy(s):
        return pltpu.make_async_remote_copy(
            send1.at[s],
            recv1.at[s],
            send1_sem.at[s],
            recv1_sem.at[s],
            device_id=(dp, example(s)),
            device_id_type=MESH,
        )

    def query_copy(i):
        d = lax.rem(dp + i, ndp)
        return pltpu.make_async_remote_copy(
            query_hbm.at[:, query_cols(d)],
            queries.at[dp],
            query_send,
            query_recv,
            device_id=(d, t),
            device_id_type=MESH,
        )

    for s in range(nt - 1):
        send1[s] = partial_of(s)
        if s == 0:
            pl.semaphore_wait(barrier, ndev - 1)
        reduce_copy(s).start()
        if s == 0:

            def send_query(i, c):
                query_copy(i).start()
                return c

            lax.fori_loop(1, ndp, send_query, 0)
    joined = partial_of(nt - 1)
    for s in range(nt - 1):
        reduce_copy(s).wait_recv()
        joined = joined + recv1[s]

    rows = lax.broadcasted_iota(jnp.int32, (seq, rank), 0)
    in_proj = jnp.where(rows < length_ref[t], joined[:, :rank], 0.0)
    tg_ref[...] = lax.dot_general(
        in_proj,
        joined[:, rank:],
        (((0,), (0,)), ((), ())),
        precision=lax.Precision.HIGHEST,
        preferred_element_type=jnp.float32,
    )
    per_slice = LANES // rank
    flat = jnp.concatenate(
        [tg_ref[pl.ds(r, slices, stride=per_slice), :] for r in range(per_slice)], axis=1
    )
    norm = jnp.sum(flat * flat, axis=0, keepdims=True)
    send2[:, 0, :] = flat
    send2[:, 1, :] = jnp.broadcast_to(norm, (slices, LANES))

    my_slot = slot_of(dp, t)
    my_slice = slice_of(dp, t)

    def grads_copy(i):
        d, x = peer(i)
        return pltpu.make_async_remote_copy(
            send2.at[slice_of(d, x)],
            recv2.at[my_slot],
            send2_sem,
            recv2_sem,
            device_id=(d, x),
            device_id_type=MESH,
        )

    def send_grads(i, c):
        grads_copy(i).start()
        return c

    lax.fori_loop(1, ndev, send_grads, 0)
    recv2[my_slot] = send2[my_slice]
    own_query.wait()
    others = queries.at[pl.ds(0, ndp - 1)]
    pltpu.make_async_copy(others, others, query_recv).wait()
    others = recv2.at[pl.ds(0, ndev - 1)]
    pltpu.make_async_copy(others, others, recv2_sem).wait()

    everyone = recv2[...]
    examples = ndp * nt
    moment = jnp.sum(everyone * everyone, axis=0)[0:1] / examples
    norms = jnp.sum(everyone, axis=0)[1:2]
    mean = jnp.sum(norms, axis=1, keepdims=True) / (examples * rank * rank)
    precond = 1.0 / (moment + DAMPING * mean)
    first = pl.multiple_of((dp // group) * slices, slices)
    grads = recv2[pl.ds(first, slices), 0, :]
    scores = contract_last(
        grads * precond, queries[...].reshape(nq, LANES), precision=lax.Precision.HIGHEST
    )
    block = slices // pack
    packed = jnp.concatenate([scores[r * block : (r + 1) * block] for r in range(pack)], axis=1)
    for d in range(group):
        send3[d] = packed[d * per_row : (d + 1) * per_row]

    my_group = dp // group

    def scores_copy(i):
        p = lax.rem(my_slice + i, slices)
        d, x = p // nt, lax.rem(p, nt)
        return pltpu.make_async_remote_copy(
            send3.at[d],
            recv3.at[my_slice],
            send3_sem,
            recv3_sem,
            device_id=(my_group * group + d, x),
            device_id_type=MESH,
        )

    def send_scores(i, c):
        scores_copy(i).start()
        return c

    lax.fori_loop(1, slices, send_scores, 0)
    recv3[my_slice] = send3[lax.rem(dp, group)]
    others = recv3.at[pl.ds(0, slices - 1)]
    pltpu.make_async_copy(others, others, recv3_sem).wait()
    total = jnp.sum(recv3[...], axis=0) * (1.0 / rank)
    for r in range(per_row):
        for c in range(pack):
            row = r * pack + c
            out_ref[row : row + 1, :] = total[r : r + 1, c * nq : (c + 1) * nq]

    for s in range(nt - 1):
        reduce_copy(s).wait_send()
    others = queries.at[pl.ds(0, ndp - 1)]
    pltpu.make_async_copy(others, others, query_send).wait()
    others = recv2.at[pl.ds(0, ndev - 1)]
    pltpu.make_async_copy(others, others, send2_sem).wait()
    others = recv3.at[pl.ds(0, slices - 1)]
    pltpu.make_async_copy(others, others, send3_sem).wait()


def per_device(
    ndp, nt, gate_pre, up_pre, out_grad, lengths, proj_hidden, proj_out, query_grads
):
    e_dev, seq, ff = gate_pre.shape
    feats = out_grad.shape[2]
    rank = proj_hidden.shape[1]
    q_dev = query_grads.shape[0]
    nq = q_dev * ndp
    slices = rank * rank // LANES
    group = slices // nt
    assert e_dev == nt and slices % nt == 0 and ndp % group == 0
    pack = max(1, LANES // nq)
    per_row = nt // pack
    halves = 2
    f32, bf16 = jnp.float32, jnp.bfloat16
    dma = pltpu.SemaphoreType.DMA
    anywhere = pl.BlockSpec(memory_space=pl.ANY)
    return pl.pallas_call(
        functools.partial(kernel, ndp, nt),
        out_shape=jax.ShapeDtypeStruct((e_dev, nq), f32),
        in_specs=[pl.BlockSpec(memory_space=pltpu.SMEM)] + [anywhere] * 6,
        out_specs=pl.BlockSpec(memory_space=pltpu.VMEM),
        scratch_shapes=[
            pltpu.VMEM((e_dev, seq, ff), bf16),
            pltpu.VMEM((e_dev, seq, ff), bf16),
            pltpu.VMEM((e_dev, seq, feats), bf16),
            pltpu.VMEM((rank, ff), bf16),
            pltpu.VMEM((rank, feats), bf16),
            pltpu.VMEM((ndp, q_dev, LANES), f32),
            pltpu.VMEM((nt - 1, seq, 2 * rank), f32),
            pltpu.VMEM((nt - 1, seq, 2 * rank), f32),
            pltpu.VMEM((rank, rank), f32),
            pltpu.VMEM((slices, 2, LANES), f32),
            pltpu.VMEM((ndp * nt, 2, LANES), f32),
            pltpu.VMEM((group, per_row, pack * nq), f32),
            pltpu.VMEM((slices, per_row, pack * nq), f32),
            dma((e_dev, halves)),
            dma((e_dev, halves)),
            dma((e_dev,)),
            dma((halves,)),
            dma,
            dma,
            dma,
            dma,
            dma((nt - 1,)),
            dma((nt - 1,)),
            dma,
            dma,
            dma,
            dma,
        ],
        compiler_params=pltpu.CompilerParams(
            collective_id=0, has_side_effects=True, vmem_limit_bytes=48 * 1024 * 1024
        ),
        cost_estimate=pl.CostEstimate(
            flops=2 * e_dev * seq * (ff + feats) * rank,
            bytes_accessed=4 * e_dev * seq * ff + 2 * e_dev * seq * feats,
            transcendentals=e_dev * seq * ff,
        ),
    )(lengths, gate_pre, up_pre, out_grad, proj_hidden.T, proj_out.T, query_grads)


def solution(mesh):
    in_specs = (
        P("dp", None, "tensor"),
        P("dp", None, "tensor"),
        P("dp", None, "tensor"),
        P("dp"),
        P("tensor", None),
        P("tensor", None),
        P("dp", None),
    )
    return jax.shard_map(
        functools.partial(per_device, mesh.shape["dp"], mesh.shape["tensor"]),
        mesh=mesh,
        in_specs=in_specs,
        out_specs=P("dp", None),
        check_vma=False,
    )
```

```python
import functools

import jax
import jax.numpy as jnp
from jax import lax
from jax.experimental import pallas as pl
from jax.experimental.pallas import tpu as pltpu
from jax.sharding import PartitionSpec as P

MESH = pl.DeviceIdType.MESH
LANES = 128
DAMPING = 0.1


def contract_last(a, b, precision=None):
    return lax.dot_general(
        a, b, (((1,), (1,)), ((), ())), precision=precision, preferred_element_type=jnp.float32
    )


def pieces(size, most):
    count = -(-size // most)
    while size % (count * LANES):
        count += 1
    return count, size // count


def kernel(
    ndp,
    nt,
    length_hbm,
    gate_hbm,
    up_hbm,
    grad_hbm,
    wh_hbm,
    wo_hbm,
    query_hbm,
    out_ref,
    length_ref,
    gate,
    up,
    grad,
    wh,
    wo,
    queries,
    send1,
    recv1,
    tg_ref,
    send2,
    recv2,
    send3,
    recv3,
    length_sem,
    gate_sem,
    up_sem,
    grad_sem,
    wh_sem,
    wo_sem,
    query_sem,
    query_send,
    query_recv,
    send1_sem,
    recv1_sem,
    send2_sem,
    recv2_sem,
    send3_sem,
    recv3_sem,
):
    seq = gate.shape[1]
    rank = wh.shape[0]
    halves, half = gate_sem.shape[1], gate.shape[2] // gate_sem.shape[1]
    feats = grad.shape[2]
    slices = rank * rank // LANES
    group = slices // nt
    ndev = ndp * nt
    nq = queries.shape[0] * queries.shape[1]
    pack = max(1, LANES // nq)
    per_row = nt // pack

    dp = lax.axis_index("dp")
    t = lax.axis_index("tensor")
    me = dp * nt + t

    def slice_of(d, x):
        return lax.rem(d, group) * nt + x

    def slot_of(d, x):
        g, local = d // group, lax.rem(d, group)
        return g * slices + lax.rem(x, pack) * (slices // pack) + local * per_row + x // pack

    def peer(i):
        p = lax.rem(me + i, ndev)
        return p // nt, lax.rem(p, nt)

    def example(s):
        return lax.rem(t + 1 + s, nt)

    barrier = pltpu.get_barrier_semaphore()

    def greet(i, c):
        pl.semaphore_signal(barrier, inc=1, device_id=peer(i), device_id_type=MESH)
        return c

    def gate_copy(e, h):
        cols = pl.ds(h * half, half)
        return pltpu.make_async_copy(
            gate_hbm.at[e, :, cols], gate.at[e, :, cols], gate_sem.at[e, h]
        )

    def up_copy(e, h):
        cols = pl.ds(h * half, half)
        return pltpu.make_async_copy(up_hbm.at[e, :, cols], up.at[e, :, cols], up_sem.at[e, h])

    def grad_copy(e):
        return pltpu.make_async_copy(grad_hbm.at[e], grad.at[e], grad_sem.at[e])

    def wh_copy(h):
        cols = pl.ds(h * half, half)
        return pltpu.make_async_copy(wh_hbm.at[:, cols], wh.at[:, cols], wh_sem.at[h])

    def query_cols(d):
        return pl.ds(pl.multiple_of(slice_of(d, t) * LANES, LANES), LANES)

    length_copy = pltpu.make_async_copy(length_hbm, length_ref, length_sem)
    wo_copy = pltpu.make_async_copy(wo_hbm, wo, wo_sem)
    own_query = pltpu.make_async_copy(query_hbm.at[:, query_cols(dp)], queries.at[dp], query_sem)

    wo_copy.start()
    for s in range(nt):
        e = example(s)
        grad_copy(e).start()
        for h in range(halves):
            if s == 0:
                wh_copy(h).start()
            gate_copy(e, h).start()
            up_copy(e, h).start()
    own_query.start()
    length_copy.start()
    lax.fori_loop(1, ndev, greet, 0)
    wo_copy.wait()

    def partial_of(s):
        e = example(s)
        grad_copy(e).wait()
        out_part = contract_last(grad[e], wo[...])
        in_part = jnp.zeros((seq, rank), jnp.float32)
        for h in range(halves):
            if s == 0:
                wh_copy(h).wait()
            gate_copy(e, h).wait()
            up_copy(e, h).wait()
            count, width = pieces(half, 512)
            for c in range(count):
                cols = pl.ds(h * half + c * width, width)
                a = gate[e, :, cols].astype(jnp.float32) * 0.5
                u = up[e, :, cols].astype(jnp.float32)
                hidden = (u * (a + a * jnp.tanh(a))).astype(jnp.bfloat16)
                in_part = in_part + contract_last(hidden, wh[:, cols])
        return jnp.concatenate([in_part, out_part], axis=1)

    def reduce_copy(s):
        return pltpu.make_async_remote_copy(
            send1.at[s],
            recv1.at[s],
            send1_sem.at[s],
            recv1_sem.at[s],
            device_id=(dp, example(s)),
            device_id_type=MESH,
        )

    def query_copy(i):
        d = lax.rem(dp + i, ndp)
        return pltpu.make_async_remote_copy(
            query_hbm.at[:, query_cols(d)],
            queries.at[dp],
            query_send,
            query_recv,
            device_id=(d, t),
            device_id_type=MESH,
        )

    for s in range(nt - 1):
        send1[s] = partial_of(s)
        if s == 0:
            pl.semaphore_wait(barrier, ndev - 1)
        reduce_copy(s).start()
        if s == 0:

            def send_query(i, c):
                query_copy(i).start()
                return c

            lax.fori_loop(1, ndp, send_query, 0)
    joined = partial_of(nt - 1)
    for s in range(nt - 1):
        reduce_copy(s).wait_recv()
        joined = joined + recv1[s]

    length_copy.wait()
    rows = lax.broadcasted_iota(jnp.int32, (seq, rank), 0)
    in_proj = jnp.where(rows < length_ref[t], joined[:, :rank], 0.0)
    tg_ref[...] = lax.dot_general(
        in_proj,
        joined[:, rank:],
        (((0,), (0,)), ((), ())),
        precision=lax.Precision.HIGHEST,
        preferred_element_type=jnp.float32,
    )
    per_slice = LANES // rank
    flat = jnp.concatenate(
        [tg_ref[pl.ds(r, slices, stride=per_slice), :] for r in range(per_slice)], axis=1
    )
    norm = jnp.sum(flat * flat, axis=0, keepdims=True)
    send2[:, 0, :] = flat
    send2[:, 1, :] = jnp.broadcast_to(norm, (slices, LANES))

    my_slot = slot_of(dp, t)
    my_slice = slice_of(dp, t)

    def grads_copy(i):
        d, x = peer(i)
        return pltpu.make_async_remote_copy(
            send2.at[slice_of(d, x)],
            recv2.at[my_slot],
            send2_sem,
            recv2_sem,
            device_id=(d, x),
            device_id_type=MESH,
        )

    def send_grads(i, c):
        grads_copy(i).start()
        return c

    lax.fori_loop(1, ndev, send_grads, 0)
    recv2[my_slot] = send2[my_slice]
    own_query.wait()
    others = queries.at[pl.ds(0, ndp - 1)]
    pltpu.make_async_copy(others, others, query_recv).wait()
    others = recv2.at[pl.ds(0, ndev - 1)]
    pltpu.make_async_copy(others, others, recv2_sem).wait()

    everyone = recv2[...]
    examples = ndp * nt
    moment = jnp.sum(everyone * everyone, axis=0)[0:1] / examples
    norms = jnp.sum(everyone, axis=0)[1:2]
    mean = jnp.sum(norms, axis=1, keepdims=True) / (examples * rank * rank)
    precond = 1.0 / (moment + DAMPING * mean)
    first = pl.multiple_of((dp // group) * slices, slices)
    grads = recv2[pl.ds(first, slices), 0, :]
    scores = contract_last(
        grads * precond, queries[...].reshape(nq, LANES), precision=lax.Precision.HIGHEST
    )
    block = slices // pack
    packed = jnp.concatenate([scores[r * block : (r + 1) * block] for r in range(pack)], axis=1)
    for d in range(group):
        send3[d] = packed[d * per_row : (d + 1) * per_row]

    my_group = dp // group

    def scores_copy(i):
        p = lax.rem(my_slice + i, slices)
        d, x = p // nt, lax.rem(p, nt)
        return pltpu.make_async_remote_copy(
            send3.at[d],
            recv3.at[my_slice],
            send3_sem,
            recv3_sem,
            device_id=(my_group * group + d, x),
            device_id_type=MESH,
        )

    def send_scores(i, c):
        scores_copy(i).start()
        return c

    lax.fori_loop(1, slices, send_scores, 0)
    recv3[my_slice] = send3[lax.rem(dp, group)]
    others = recv3.at[pl.ds(0, slices - 1)]
    pltpu.make_async_copy(others, others, recv3_sem).wait()
    total = jnp.sum(recv3[...], axis=0) * (1.0 / rank)
    for r in range(per_row):
        for c in range(pack):
            row = r * pack + c
            out_ref[row : row + 1, :] = total[r : r + 1, c * nq : (c + 1) * nq]

    for s in range(nt - 1):
        reduce_copy(s).wait_send()
    others = queries.at[pl.ds(0, ndp - 1)]
    pltpu.make_async_copy(others, others, query_send).wait()
    others = recv2.at[pl.ds(0, ndev - 1)]
    pltpu.make_async_copy(others, others, send2_sem).wait()
    others = recv3.at[pl.ds(0, slices - 1)]
    pltpu.make_async_copy(others, others, send3_sem).wait()


def per_device(
    ndp, nt, gate_pre, up_pre, out_grad, lengths, proj_hidden, proj_out, query_grads
):
    e_dev, seq, ff = gate_pre.shape
    feats = out_grad.shape[2]
    rank = proj_hidden.shape[1]
    q_dev = query_grads.shape[0]
    nq = q_dev * ndp
    slices = rank * rank // LANES
    group = slices // nt
    assert e_dev == nt and slices % nt == 0 and ndp % group == 0
    pack = max(1, LANES // nq)
    per_row = nt // pack
    halves = 2
    f32, bf16 = jnp.float32, jnp.bfloat16
    dma = pltpu.SemaphoreType.DMA
    in_hbm = pl.BlockSpec(memory_space=pl.ANY)
    return pl.pallas_call(
        functools.partial(kernel, ndp, nt),
        out_shape=jax.ShapeDtypeStruct((e_dev, nq), f32),
        in_specs=[in_hbm] * 7,
        out_specs=pl.BlockSpec(memory_space=pltpu.VMEM),
        scratch_shapes=[
            pltpu.SMEM((e_dev,), jnp.int32),
            pltpu.VMEM((e_dev, seq, ff), bf16),
            pltpu.VMEM((e_dev, seq, ff), bf16),
            pltpu.VMEM((e_dev, seq, feats), bf16),
            pltpu.VMEM((rank, ff), bf16),
            pltpu.VMEM((rank, feats), bf16),
            pltpu.VMEM((ndp, q_dev, LANES), f32),
            pltpu.VMEM((nt - 1, seq, 2 * rank), f32),
            pltpu.VMEM((nt - 1, seq, 2 * rank), f32),
            pltpu.VMEM((rank, rank), f32),
            pltpu.VMEM((slices, 2, LANES), f32),
            pltpu.VMEM((ndp * nt, 2, LANES), f32),
            pltpu.VMEM((group, per_row, pack * nq), f32),
            pltpu.VMEM((slices, per_row, pack * nq), f32),
            dma,
            dma((e_dev, halves)),
            dma((e_dev, halves)),
            dma((e_dev,)),
            dma((halves,)),
            dma,
            dma,
            dma,
            dma,
            dma((nt - 1,)),
            dma((nt - 1,)),
            dma,
            dma,
            dma,
            dma,
        ],
        compiler_params=pltpu.CompilerParams(
            collective_id=0, has_side_effects=True, vmem_limit_bytes=64 * 1024 * 1024
        ),
        cost_estimate=pl.CostEstimate(
            flops=2 * e_dev * seq * (ff + feats) * rank,
            bytes_accessed=4 * e_dev * seq * ff + 2 * e_dev * seq * feats,
            transcendentals=e_dev * seq * ff,
        ),
    )(lengths, gate_pre, up_pre, out_grad, proj_hidden.T, proj_out.T, query_grads)


def solution(mesh):
    in_specs = (
        P("dp", None, "tensor"),
        P("dp", None, "tensor"),
        P("dp", None, "tensor"),
        P("dp"),
        P("tensor", None),
        P("tensor", None),
        P("dp", None),
    )
    return jax.shard_map(
        functools.partial(per_device, mesh.shape["dp"], mesh.shape["tensor"]),
        mesh=mesh,
        in_specs=in_specs,
        out_specs=P("dp", None),
        check_vma=False,
    )
```

```python
import functools

import jax
import jax.numpy as jnp
from jax import lax
from jax.experimental import pallas as pl
from jax.experimental.pallas import tpu as pltpu
from jax.sharding import PartitionSpec as P

MESH = pl.DeviceIdType.MESH
LANES = 128
DAMPING = 0.1


def contract_last(a, b):
    return lax.dot_general(
        a, b, (((1,), (1,)), ((), ())), preferred_element_type=jnp.float32
    )


def high_low(v):
    high = v.astype(jnp.bfloat16)
    return high, (v - high.astype(jnp.float32)).astype(jnp.bfloat16)


def left_terms(v, axis):
    high, low = high_low(v)
    return jnp.concatenate([high, high, low], axis=axis)


def right_terms(v, axis):
    high, low = high_low(v)
    return jnp.concatenate([high, low, high], axis=axis)


def each(count, body, block=8):
    full = count // block

    def several(b, c):
        for j in range(block):
            body(1 + b * block + j)
        return c

    if full:
        lax.fori_loop(0, full, several, 0)
    for j in range(full * block, count):
        body(1 + j)


def pieces(size, most):
    count = -(-size // most)
    while size % (count * LANES):
        count += 1
    return count, size // count


def kernel(
    ndp,
    nt,
    length_hbm,
    gate_hbm,
    up_hbm,
    grad_hbm,
    wh_hbm,
    wo_hbm,
    query_hbm,
    out_ref,
    length_ref,
    gate,
    up,
    grad,
    wh,
    wo,
    queries,
    send1,
    recv1,
    tg_ref,
    send2,
    recv2,
    send3,
    recv3,
    length_sem,
    gate_sem,
    up_sem,
    grad_sem,
    wh_sem,
    wo_sem,
    query_sem,
    query_send,
    query_recv,
    send1_sem,
    recv1_sem,
    send2_sem,
    recv2_sem,
    send3_sem,
    recv3_sem,
):
    seq = gate.shape[1]
    rank = wh.shape[0]
    halves, half = gate_sem.shape[1], gate.shape[2] // gate_sem.shape[1]
    feats = grad.shape[2]
    slices = rank * rank // LANES
    group = slices // nt
    ndev = ndp * nt
    nq = queries.shape[0] * queries.shape[1]
    pack = max(1, LANES // nq)
    per_row = nt // pack

    dp = lax.axis_index("dp")
    t = lax.axis_index("tensor")
    me = dp * nt + t

    def within(d):
        return d if group == ndp else lax.rem(d, group)

    def slice_of(d, x):
        return within(d) * nt + x

    def slot_of(d, x):
        g, local = lax.div(d, group), within(d)
        place = lax.rem(x, pack) * (slices // pack) + local * per_row + lax.div(x, pack)
        return g * slices + place

    def peer(i):
        p = lax.rem(me + i, ndev)
        return lax.div(p, nt), lax.rem(p, nt)

    def example(s):
        return lax.rem(t + 1 + s, nt)

    barrier = pltpu.get_barrier_semaphore()

    def greet(i):
        pl.semaphore_signal(barrier, inc=1, device_id=peer(i), device_id_type=MESH)

    def gate_copy(e, h):
        cols = pl.ds(h * half, half)
        return pltpu.make_async_copy(
            gate_hbm.at[e, :, cols], gate.at[e, :, cols], gate_sem.at[e, h]
        )

    def up_copy(e, h):
        cols = pl.ds(h * half, half)
        return pltpu.make_async_copy(up_hbm.at[e, :, cols], up.at[e, :, cols], up_sem.at[e, h])

    def grad_copy(e):
        return pltpu.make_async_copy(grad_hbm.at[e], grad.at[e], grad_sem.at[e])

    def wh_copy(h):
        cols = pl.ds(h * half, half)
        return pltpu.make_async_copy(wh_hbm.at[:, cols], wh.at[:, cols], wh_sem.at[h])

    def query_cols(d):
        return pl.ds(pl.multiple_of(slice_of(d, t) * LANES, LANES), LANES)

    length_copy = pltpu.make_async_copy(length_hbm, length_ref, length_sem)
    wo_copy = pltpu.make_async_copy(wo_hbm, wo, wo_sem)
    own_query = pltpu.make_async_copy(query_hbm.at[:, query_cols(dp)], queries.at[dp], query_sem)

    wo_copy.start()
    for s in range(nt):
        e = example(s)
        grad_copy(e).start()
        for h in range(halves):
            if s == 0:
                wh_copy(h).start()
            gate_copy(e, h).start()
            up_copy(e, h).start()
    own_query.start()
    length_copy.start()
    each(ndev - 1, greet)
    wo_copy.wait()

    def partial_of(s):
        e = example(s)
        grad_copy(e).wait()
        out_part = contract_last(grad[e], wo[...])
        in_part = jnp.zeros((seq, rank), jnp.float32)
        for h in range(halves):
            if s == 0:
                wh_copy(h).wait()
            gate_copy(e, h).wait()
            up_copy(e, h).wait()
            count, width = pieces(half, 512)
            for c in range(count):
                cols = pl.ds(h * half + c * width, width)
                a = gate[e, :, cols].astype(jnp.float32) * 0.5
                u = up[e, :, cols].astype(jnp.float32)
                hidden = (u * (a + a * jnp.tanh(a))).astype(jnp.bfloat16)
                in_part = in_part + contract_last(hidden, wh[:, cols])
        return jnp.concatenate([in_part, out_part], axis=1)

    def reduce_copy(s):
        return pltpu.make_async_remote_copy(
            send1.at[s],
            recv1.at[s],
            send1_sem.at[s],
            recv1_sem.at[s],
            device_id=(dp, example(s)),
            device_id_type=MESH,
        )

    def query_copy(i):
        d = lax.rem(dp + i, ndp)
        return pltpu.make_async_remote_copy(
            query_hbm.at[:, query_cols(d)],
            queries.at[dp],
            query_send,
            query_recv,
            device_id=(d, t),
            device_id_type=MESH,
        )

    for s in range(nt - 1):
        send1[s] = partial_of(s)
        if s == 0:
            pl.semaphore_wait(barrier, ndev - 1)
        reduce_copy(s).start()
        if s == 0:
            each(ndp - 1, lambda i: query_copy(i).start())
    joined = partial_of(nt - 1)
    for s in range(nt - 1):
        reduce_copy(s).wait_recv()
        joined = joined + recv1[s]

    length_copy.wait()
    rows = lax.broadcasted_iota(jnp.int32, (seq, rank), 0)
    in_proj = jnp.where(rows < length_ref[t], joined[:, :rank], 0.0)
    tg_ref[...] = lax.dot_general(
        left_terms(in_proj, 0),
        right_terms(joined[:, rank:], 0),
        (((0,), (0,)), ((), ())),
        preferred_element_type=jnp.float32,
    )
    per_slice = LANES // rank
    flat = jnp.concatenate(
        [tg_ref[pl.ds(r, slices, stride=per_slice), :] for r in range(per_slice)], axis=1
    )
    norm = jnp.sum(flat * flat, axis=0, keepdims=True)
    send2[:, 0, :] = flat
    send2[:, 1, :] = jnp.broadcast_to(norm, (slices, LANES))

    my_slot = slot_of(dp, t)
    my_slice = slice_of(dp, t)

    def grads_copy(i):
        d, x = peer(i)
        return pltpu.make_async_remote_copy(
            send2.at[slice_of(d, x)],
            recv2.at[my_slot],
            send2_sem,
            recv2_sem,
            device_id=(d, x),
            device_id_type=MESH,
        )

    each(ndev - 1, lambda i: grads_copy(i).start())
    recv2[my_slot] = send2[my_slice]
    own_query.wait()
    others = queries.at[pl.ds(0, ndp - 1)]
    pltpu.make_async_copy(others, others, query_recv).wait()
    query_terms = right_terms(queries[...].reshape(nq, LANES), 1)
    others = recv2.at[pl.ds(0, ndev - 1)]
    pltpu.make_async_copy(others, others, recv2_sem).wait()

    everyone = recv2[...]
    examples = ndp * nt
    moment = jnp.sum(everyone * everyone, axis=0)[0:1] / examples
    norms = jnp.sum(everyone, axis=0)[1:2]
    mean = jnp.sum(norms, axis=1, keepdims=True) / (examples * rank * rank)
    precond = 1.0 / (moment + DAMPING * mean)
    first = pl.multiple_of(lax.div(dp, group) * slices, slices)
    grads = recv2[pl.ds(first, slices), 0, :]
    scores = contract_last(left_terms(grads * precond, 1), query_terms)
    block = slices // pack
    packed = jnp.concatenate([scores[r * block : (r + 1) * block] for r in range(pack)], axis=1)
    for d in range(group):
        send3[d] = packed[d * per_row : (d + 1) * per_row]

    my_group = lax.div(dp, group)

    def scores_copy(i):
        p = lax.rem(my_slice + i, slices)
        d, x = lax.div(p, nt), lax.rem(p, nt)
        return pltpu.make_async_remote_copy(
            send3.at[d],
            recv3.at[my_slice],
            send3_sem,
            recv3_sem,
            device_id=(my_group * group + d, x),
            device_id_type=MESH,
        )

    each(slices - 1, lambda i: scores_copy(i).start())
    recv3[my_slice] = send3[within(dp)]
    others = recv3.at[pl.ds(0, slices - 1)]
    pltpu.make_async_copy(others, others, recv3_sem).wait()
    total = jnp.sum(recv3[...], axis=0) * (1.0 / rank)
    for r in range(per_row):
        for c in range(pack):
            row = r * pack + c
            out_ref[row : row + 1, :] = total[r : r + 1, c * nq : (c + 1) * nq]

    for s in range(nt - 1):
        reduce_copy(s).wait_send()
    others = queries.at[pl.ds(0, ndp - 1)]
    pltpu.make_async_copy(others, others, query_send).wait()
    others = recv2.at[pl.ds(0, ndev - 1)]
    pltpu.make_async_copy(others, others, send2_sem).wait()
    others = recv3.at[pl.ds(0, slices - 1)]
    pltpu.make_async_copy(others, others, send3_sem).wait()


def per_device(
    ndp, nt, gate_pre, up_pre, out_grad, lengths, proj_hidden, proj_out, query_grads
):
    e_dev, seq, ff = gate_pre.shape
    feats = out_grad.shape[2]
    rank = proj_hidden.shape[1]
    q_dev = query_grads.shape[0]
    nq = q_dev * ndp
    slices = rank * rank // LANES
    group = slices // nt
    assert e_dev == nt and slices % nt == 0 and ndp % group == 0
    pack = max(1, LANES // nq)
    per_row = nt // pack
    halves = 2
    f32, bf16 = jnp.float32, jnp.bfloat16
    dma = pltpu.SemaphoreType.DMA
    in_hbm = pl.BlockSpec(memory_space=pl.ANY)
    return pl.pallas_call(
        functools.partial(kernel, ndp, nt),
        out_shape=jax.ShapeDtypeStruct((e_dev, nq), f32),
        in_specs=[in_hbm] * 7,
        out_specs=pl.BlockSpec(memory_space=pltpu.VMEM),
        scratch_shapes=[
            pltpu.SMEM((e_dev,), jnp.int32),
            pltpu.VMEM((e_dev, seq, ff), bf16),
            pltpu.VMEM((e_dev, seq, ff), bf16),
            pltpu.VMEM((e_dev, seq, feats), bf16),
            pltpu.VMEM((rank, ff), bf16),
            pltpu.VMEM((rank, feats), bf16),
            pltpu.VMEM((ndp, q_dev, LANES), f32),
            pltpu.VMEM((nt - 1, seq, 2 * rank), f32),
            pltpu.VMEM((nt - 1, seq, 2 * rank), f32),
            pltpu.VMEM((rank, rank), f32),
            pltpu.VMEM((slices, 2, LANES), f32),
            pltpu.VMEM((ndp * nt, 2, LANES), f32),
            pltpu.VMEM((group, per_row, pack * nq), f32),
            pltpu.VMEM((slices, per_row, pack * nq), f32),
            dma,
            dma((e_dev, halves)),
            dma((e_dev, halves)),
            dma((e_dev,)),
            dma((halves,)),
            dma,
            dma,
            dma,
            dma,
            dma((nt - 1,)),
            dma((nt - 1,)),
            dma,
            dma,
            dma,
            dma,
        ],
        compiler_params=pltpu.CompilerParams(
            collective_id=0, has_side_effects=True, vmem_limit_bytes=64 * 1024 * 1024
        ),
        cost_estimate=pl.CostEstimate(
            flops=2 * e_dev * seq * (ff + feats) * rank,
            bytes_accessed=4 * e_dev * seq * ff + 2 * e_dev * seq * feats,
            transcendentals=e_dev * seq * ff,
        ),
    )(lengths, gate_pre, up_pre, out_grad, proj_hidden.T, proj_out.T, query_grads)


def solution(mesh):
    in_specs = (
        P("dp", None, "tensor"),
        P("dp", None, "tensor"),
        P("dp", None, "tensor"),
        P("dp"),
        P("tensor", None),
        P("tensor", None),
        P("dp", None),
    )
    return jax.shard_map(
        functools.partial(per_device, mesh.shape["dp"], mesh.shape["tensor"]),
        mesh=mesh,
        in_specs=in_specs,
        out_specs=P("dp", None),
        check_vma=False,
    )
```

```python
import functools

import jax
import jax.numpy as jnp
from jax import lax
from jax.experimental import pallas as pl
from jax.experimental.pallas import tpu as pltpu
from jax.sharding import PartitionSpec as P

MESH = pl.DeviceIdType.MESH
LANES = 128
DAMPING = 0.1


def contract_last(a, b):
    return lax.dot_general(
        a, b, (((1,), (1,)), ((), ())), preferred_element_type=jnp.float32
    )


def high_low(v):
    high = v.astype(jnp.bfloat16)
    return high, (v - high.astype(jnp.float32)).astype(jnp.bfloat16)


def left_terms(v, axis):
    high, low = high_low(v)
    return jnp.concatenate([high, high, low], axis=axis)


def right_terms(v, axis):
    high, low = high_low(v)
    return jnp.concatenate([high, low, high], axis=axis)


def each(count, body, block=8):
    full = count // block

    def several(b, c):
        for j in range(block):
            body(1 + b * block + j)
        return c

    if full:
        lax.fori_loop(0, full, several, 0)
    for j in range(full * block, count):
        body(1 + j)


def pieces(size, most):
    count = -(-size // most)
    while size % (count * LANES):
        count += 1
    return count, size // count


def kernel(
    ndp,
    nt,
    length_hbm,
    gate_hbm,
    up_hbm,
    grad_hbm,
    wh_hbm,
    wo_hbm,
    query_hbm,
    out_ref,
    length_ref,
    gate,
    up,
    grad,
    wh,
    wo,
    queries,
    send1,
    recv1,
    tg_ref,
    send2,
    recv2,
    send3,
    recv3,
    length_sem,
    gate_sem,
    up_sem,
    grad_sem,
    wh_sem,
    wo_sem,
    query_sem,
    query_send,
    query_recv,
    send1_sem,
    recv1_sem,
    send2_sem,
    recv2_sem,
    send3_sem,
    recv3_sem,
):
    seq = gate.shape[1]
    rank = wh.shape[0]
    halves, half = gate_sem.shape[1], gate.shape[2] // gate_sem.shape[1]
    feats = grad.shape[2]
    slices = rank * rank // LANES
    group = slices // nt
    ndev = ndp * nt
    nq = queries.shape[0] * queries.shape[1]
    pack = max(1, LANES // nq)
    per_row = nt // pack

    dp = lax.axis_index("dp")
    t = lax.axis_index("tensor")
    me = dp * nt + t

    def within(d):
        return d if group == ndp else lax.rem(d, group)

    def slice_of(d, x):
        return within(d) * nt + x

    def slot_of(d, x):
        g, local = lax.div(d, group), within(d)
        place = lax.rem(x, pack) * (slices // pack) + local * per_row + lax.div(x, pack)
        return g * slices + place

    def peer(i):
        p = lax.rem(me + i, ndev)
        return lax.div(p, nt), lax.rem(p, nt)

    def example(s):
        return lax.rem(t + 1 + s, nt)

    barrier = pltpu.get_barrier_semaphore()

    def greet(i):
        pl.semaphore_signal(barrier, inc=1, device_id=peer(i), device_id_type=MESH)

    def gate_copy(e, h):
        cols = pl.ds(h * half, half)
        return pltpu.make_async_copy(
            gate_hbm.at[e, :, cols], gate.at[e, :, cols], gate_sem.at[e, h]
        )

    def up_copy(e, h):
        cols = pl.ds(h * half, half)
        return pltpu.make_async_copy(up_hbm.at[e, :, cols], up.at[e, :, cols], up_sem.at[e, h])

    def grad_copy(e):
        return pltpu.make_async_copy(grad_hbm.at[e], grad.at[e], grad_sem.at[e])

    def wh_copy(h):
        cols = pl.ds(h * half, half)
        return pltpu.make_async_copy(wh_hbm.at[:, cols], wh.at[:, cols], wh_sem.at[h])

    def query_cols(d):
        return pl.ds(pl.multiple_of(slice_of(d, t) * LANES, LANES), LANES)

    length_copy = pltpu.make_async_copy(length_hbm, length_ref, length_sem)
    wo_copy = pltpu.make_async_copy(wo_hbm, wo, wo_sem)
    own_query = pltpu.make_async_copy(query_hbm.at[:, query_cols(dp)], queries.at[dp], query_sem)

    first_sends = min(1, nt - 2)
    wo_copy.start()
    for s in range(nt):
        e = example(s)
        grad_copy(e).start()
        for h in range(halves):
            if s == 0:
                wh_copy(h).start()
            gate_copy(e, h).start()
            up_copy(e, h).start()
        if s == first_sends:
            each(ndev - 1, greet)
    own_query.start()
    length_copy.start()
    wo_copy.wait()

    def partial_of(s):
        e = example(s)
        grad_copy(e).wait()
        out_part = contract_last(grad[e], wo[...])
        in_part = jnp.zeros((seq, rank), jnp.float32)
        for h in range(halves):
            if s == 0:
                wh_copy(h).wait()
            gate_copy(e, h).wait()
            up_copy(e, h).wait()
            count, width = pieces(half, 512)
            for c in range(count):
                cols = pl.ds(h * half + c * width, width)
                a = gate[e, :, cols].astype(jnp.float32) * 0.5
                u = up[e, :, cols].astype(jnp.float32)
                hidden = (u * (a + a * jnp.tanh(a))).astype(jnp.bfloat16)
                in_part = in_part + contract_last(hidden, wh[:, cols])
        return jnp.concatenate([in_part, out_part], axis=1)

    def reduce_copy(s):
        return pltpu.make_async_remote_copy(
            send1.at[s],
            recv1.at[s],
            send1_sem.at[s],
            recv1_sem.at[s],
            device_id=(dp, example(s)),
            device_id_type=MESH,
        )

    def query_copy(i):
        d = lax.rem(dp + i, ndp)
        return pltpu.make_async_remote_copy(
            query_hbm.at[:, query_cols(d)],
            queries.at[dp],
            query_send,
            query_recv,
            device_id=(d, t),
            device_id_type=MESH,
        )

    for s in range(nt - 1):
        send1[s] = partial_of(s)
        if s == first_sends:
            pl.semaphore_wait(barrier, ndev - 1)
            for before in range(s):
                reduce_copy(before).start()
        if s >= first_sends:
            reduce_copy(s).start()
        if s == first_sends:
            each(ndp - 1, lambda i: query_copy(i).start())
    joined = partial_of(nt - 1)
    for s in range(nt - 1):
        reduce_copy(s).wait_recv()
        joined = joined + recv1[s]

    length_copy.wait()
    rows = lax.broadcasted_iota(jnp.int32, (seq, rank), 0)
    in_proj = jnp.where(rows < length_ref[t], joined[:, :rank], 0.0)
    tg_ref[...] = lax.dot_general(
        left_terms(in_proj, 0),
        right_terms(joined[:, rank:], 0),
        (((0,), (0,)), ((), ())),
        preferred_element_type=jnp.float32,
    )
    per_slice = LANES // rank
    flat = jnp.concatenate(
        [tg_ref[pl.ds(r, slices, stride=per_slice), :] for r in range(per_slice)], axis=1
    )
    norm = jnp.sum(flat * flat, axis=0, keepdims=True)
    send2[:, 0, :] = flat
    send2[:, 1, :] = jnp.broadcast_to(norm, (slices, LANES))

    my_slot = slot_of(dp, t)
    my_slice = slice_of(dp, t)

    def grads_copy(i):
        d, x = peer(i)
        return pltpu.make_async_remote_copy(
            send2.at[slice_of(d, x)],
            recv2.at[my_slot],
            send2_sem,
            recv2_sem,
            device_id=(d, x),
            device_id_type=MESH,
        )

    each(ndev - 1, lambda i: grads_copy(i).start())
    recv2[my_slot] = send2[my_slice]
    own_query.wait()
    others = queries.at[pl.ds(0, ndp - 1)]
    pltpu.make_async_copy(others, others, query_recv).wait()
    query_terms = right_terms(queries[...].reshape(nq, LANES), 1)
    others = recv2.at[pl.ds(0, ndev - 1)]
    pltpu.make_async_copy(others, others, recv2_sem).wait()

    everyone = recv2[...]
    examples = ndp * nt
    moment = jnp.sum(everyone * everyone, axis=0)[0:1] / examples
    norms = jnp.sum(everyone, axis=0)[1:2]
    mean = jnp.sum(norms, axis=1, keepdims=True) / (examples * rank * rank)
    precond = 1.0 / (moment + DAMPING * mean)
    first = pl.multiple_of(lax.div(dp, group) * slices, slices)
    grads = recv2[pl.ds(first, slices), 0, :]
    scores = contract_last(left_terms(grads * precond, 1), query_terms)
    block = slices // pack
    packed = jnp.concatenate([scores[r * block : (r + 1) * block] for r in range(pack)], axis=1)
    for d in range(group):
        send3[d] = packed[d * per_row : (d + 1) * per_row]

    my_group = lax.div(dp, group)

    def scores_copy(i):
        p = lax.rem(my_slice + i, slices)
        d, x = lax.div(p, nt), lax.rem(p, nt)
        return pltpu.make_async_remote_copy(
            send3.at[d],
            recv3.at[my_slice],
            send3_sem,
            recv3_sem,
            device_id=(my_group * group + d, x),
            device_id_type=MESH,
        )

    each(slices - 1, lambda i: scores_copy(i).start())
    recv3[my_slice] = send3[within(dp)]
    others = recv3.at[pl.ds(0, slices - 1)]
    pltpu.make_async_copy(others, others, recv3_sem).wait()
    total = jnp.sum(recv3[...], axis=0) * (1.0 / rank)
    for r in range(per_row):
        for c in range(pack):
            row = r * pack + c
            out_ref[row : row + 1, :] = total[r : r + 1, c * nq : (c + 1) * nq]

    for s in range(nt - 1):
        reduce_copy(s).wait_send()
    others = queries.at[pl.ds(0, ndp - 1)]
    pltpu.make_async_copy(others, others, query_send).wait()
    others = recv2.at[pl.ds(0, ndev - 1)]
    pltpu.make_async_copy(others, others, send2_sem).wait()
    others = recv3.at[pl.ds(0, slices - 1)]
    pltpu.make_async_copy(others, others, send3_sem).wait()


def per_device(
    ndp, nt, gate_pre, up_pre, out_grad, lengths, proj_hidden, proj_out, query_grads
):
    e_dev, seq, ff = gate_pre.shape
    feats = out_grad.shape[2]
    rank = proj_hidden.shape[1]
    q_dev = query_grads.shape[0]
    nq = q_dev * ndp
    slices = rank * rank // LANES
    group = slices // nt
    assert e_dev == nt and slices % nt == 0 and ndp % group == 0
    pack = max(1, LANES // nq)
    per_row = nt // pack
    halves = 2
    f32, bf16 = jnp.float32, jnp.bfloat16
    dma = pltpu.SemaphoreType.DMA
    in_hbm = pl.BlockSpec(memory_space=pl.ANY)
    return pl.pallas_call(
        functools.partial(kernel, ndp, nt),
        out_shape=jax.ShapeDtypeStruct((e_dev, nq), f32),
        in_specs=[in_hbm] * 7,
        out_specs=pl.BlockSpec(memory_space=pltpu.VMEM),
        scratch_shapes=[
            pltpu.SMEM((e_dev,), jnp.int32),
            pltpu.VMEM((e_dev, seq, ff), bf16),
            pltpu.VMEM((e_dev, seq, ff), bf16),
            pltpu.VMEM((e_dev, seq, feats), bf16),
            pltpu.VMEM((rank, ff), bf16),
            pltpu.VMEM((rank, feats), bf16),
            pltpu.VMEM((ndp, q_dev, LANES), f32),
            pltpu.VMEM((nt - 1, seq, 2 * rank), f32),
            pltpu.VMEM((nt - 1, seq, 2 * rank), f32),
            pltpu.VMEM((rank, rank), f32),
            pltpu.VMEM((slices, 2, LANES), f32),
            pltpu.VMEM((ndp * nt, 2, LANES), f32),
            pltpu.VMEM((group, per_row, pack * nq), f32),
            pltpu.VMEM((slices, per_row, pack * nq), f32),
            dma,
            dma((e_dev, halves)),
            dma((e_dev, halves)),
            dma((e_dev,)),
            dma((halves,)),
            dma,
            dma,
            dma,
            dma,
            dma((nt - 1,)),
            dma((nt - 1,)),
            dma,
            dma,
            dma,
            dma,
        ],
        compiler_params=pltpu.CompilerParams(
            collective_id=0, has_side_effects=True, vmem_limit_bytes=64 * 1024 * 1024
        ),
        cost_estimate=pl.CostEstimate(
            flops=2 * e_dev * seq * (ff + feats) * rank,
            bytes_accessed=4 * e_dev * seq * ff + 2 * e_dev * seq * feats,
            transcendentals=e_dev * seq * ff,
        ),
    )(lengths, gate_pre, up_pre, out_grad, proj_hidden.T, proj_out.T, query_grads)


def solution(mesh):
    in_specs = (
        P("dp", None, "tensor"),
        P("dp", None, "tensor"),
        P("dp", None, "tensor"),
        P("dp"),
        P("tensor", None),
        P("tensor", None),
        P("dp", None),
    )
    return jax.shard_map(
        functools.partial(per_device, mesh.shape["dp"], mesh.shape["tensor"]),
        mesh=mesh,
        in_specs=in_specs,
        out_specs=P("dp", None),
        check_vma=False,
    )
```

```python
import functools

import jax
import jax.numpy as jnp
from jax import lax
from jax.experimental import pallas as pl
from jax.experimental.pallas import tpu as pltpu
from jax.sharding import PartitionSpec as P

MESH = pl.DeviceIdType.MESH
LANES = 128
DAMPING = 0.1


def contract_last(a, b):
    return lax.dot_general(
        a, b, (((1,), (1,)), ((), ())), preferred_element_type=jnp.float32
    )


def high_low(v):
    high = v.astype(jnp.bfloat16)
    return high, (v - high.astype(jnp.float32)).astype(jnp.bfloat16)


def left_terms(v, axis):
    high, low = high_low(v)
    return jnp.concatenate([high, high, low], axis=axis)


def right_terms(v, axis):
    high, low = high_low(v)
    return jnp.concatenate([high, low, high], axis=axis)


def each(count, body, block=8):
    full = count // block

    def several(b, c):
        for j in range(block):
            body(1 + b * block + j)
        return c

    if full:
        lax.fori_loop(0, full, several, 0)
    for j in range(full * block, count):
        body(1 + j)


def pieces(size, most):
    count = -(-size // most)
    while size % (count * LANES):
        count += 1
    return count, size // count


def kernel(
    ndp,
    nt,
    length_hbm,
    gate_hbm,
    up_hbm,
    grad_hbm,
    wh_hbm,
    wo_hbm,
    query_hbm,
    out_ref,
    length_ref,
    gate,
    up,
    grad,
    wh,
    wo,
    queries,
    send1,
    recv1,
    tg_ref,
    send2,
    recv2,
    send3,
    recv3,
    length_sem,
    gate_sem,
    up_sem,
    grad_sem,
    wh_sem,
    wo_sem,
    query_sem,
    query_send,
    query_recv,
    send1_sem,
    recv1_sem,
    send2_sem,
    recv2_sem,
    send3_sem,
    recv3_sem,
):
    seq = gate.shape[1]
    rank = wh.shape[0]
    halves, half = gate_sem.shape[1], gate.shape[2] // gate_sem.shape[1]
    feats = grad.shape[2]
    slices = rank * rank // LANES
    group = slices // nt
    ndev = ndp * nt
    nq = queries.shape[0] * queries.shape[1]
    pack = max(1, LANES // nq)
    per_row = nt // pack

    dp = lax.axis_index("dp")
    t = lax.axis_index("tensor")
    me = dp * nt + t

    def within(d):
        return d if group == ndp else lax.rem(d, group)

    def slice_of(d, x):
        return within(d) * nt + x

    def slot_of(d, x):
        g, local = lax.div(d, group), within(d)
        place = lax.rem(x, pack) * (slices // pack) + local * per_row + lax.div(x, pack)
        return g * slices + place

    def peer(i):
        p = lax.rem(me + i, ndev)
        return lax.div(p, nt), lax.rem(p, nt)

    def example(s):
        return lax.rem(t + 1 + s, nt)

    barrier = pltpu.get_barrier_semaphore()

    def greet(i):
        pl.semaphore_signal(barrier, inc=1, device_id=peer(i), device_id_type=MESH)

    def gate_copy(e, h):
        cols = pl.ds(h * half, half)
        return pltpu.make_async_copy(
            gate_hbm.at[e, :, cols], gate.at[e, :, cols], gate_sem.at[e, h]
        )

    def up_copy(e, h):
        cols = pl.ds(h * half, half)
        return pltpu.make_async_copy(up_hbm.at[e, :, cols], up.at[e, :, cols], up_sem.at[e, h])

    def grad_copy(e):
        return pltpu.make_async_copy(grad_hbm.at[e], grad.at[e], grad_sem.at[e])

    def wh_copy(h):
        cols = pl.ds(h * half, half)
        return pltpu.make_async_copy(wh_hbm.at[:, cols], wh.at[:, cols], wh_sem.at[h])

    def query_cols(d):
        return pl.ds(pl.multiple_of(slice_of(d, t) * LANES, LANES), LANES)

    length_copy = pltpu.make_async_copy(length_hbm, length_ref, length_sem)
    wo_copy = pltpu.make_async_copy(wo_hbm, wo, wo_sem)
    own_query = pltpu.make_async_copy(query_hbm.at[:, query_cols(dp)], queries.at[dp], query_sem)

    first_sends = nt - 2
    wo_copy.start()
    for s in range(nt):
        e = example(s)
        grad_copy(e).start()
        for h in range(halves):
            if s == 0:
                wh_copy(h).start()
            gate_copy(e, h).start()
            up_copy(e, h).start()
        if s == min(1, first_sends):
            each(ndev - 1, greet)
    own_query.start()
    length_copy.start()
    wo_copy.wait()

    def partial_of(s):
        e = example(s)
        grad_copy(e).wait()
        out_part = contract_last(grad[e], wo[...])
        in_part = jnp.zeros((seq, rank), jnp.float32)
        for h in range(halves):
            if s == 0:
                wh_copy(h).wait()
            gate_copy(e, h).wait()
            up_copy(e, h).wait()
            count, width = pieces(half, 512)
            for c in range(count):
                cols = pl.ds(h * half + c * width, width)
                a = gate[e, :, cols].astype(jnp.float32) * 0.5
                u = up[e, :, cols].astype(jnp.float32)
                hidden = (u * (a + a * jnp.tanh(a))).astype(jnp.bfloat16)
                in_part = in_part + contract_last(hidden, wh[:, cols])
        return jnp.concatenate([in_part, out_part], axis=1)

    def reduce_copy(s):
        return pltpu.make_async_remote_copy(
            send1.at[s],
            recv1.at[s],
            send1_sem.at[s],
            recv1_sem.at[s],
            device_id=(dp, example(s)),
            device_id_type=MESH,
        )

    def query_copy(i):
        d = lax.rem(dp + i, ndp)
        return pltpu.make_async_remote_copy(
            query_hbm.at[:, query_cols(d)],
            queries.at[dp],
            query_send,
            query_recv,
            device_id=(d, t),
            device_id_type=MESH,
        )

    for s in range(nt - 1):
        send1[s] = partial_of(s)
        if s == first_sends:
            pl.semaphore_wait(barrier, ndev - 1)
            for before in range(s):
                reduce_copy(before).start()
        if s >= first_sends:
            reduce_copy(s).start()
        if s == first_sends:
            each(ndp - 1, lambda i: query_copy(i).start())
    joined = partial_of(nt - 1)
    for s in range(nt - 1):
        reduce_copy(s).wait_recv()
        joined = joined + recv1[s]

    length_copy.wait()
    rows = lax.broadcasted_iota(jnp.int32, (seq, rank), 0)
    in_proj = jnp.where(rows < length_ref[t], joined[:, :rank], 0.0)
    tg_ref[...] = lax.dot_general(
        left_terms(in_proj, 0),
        right_terms(joined[:, rank:], 0),
        (((0,), (0,)), ((), ())),
        preferred_element_type=jnp.float32,
    )
    per_slice = LANES // rank
    flat = jnp.concatenate(
        [tg_ref[pl.ds(r, slices, stride=per_slice), :] for r in range(per_slice)], axis=1
    )
    norm = jnp.sum(flat * flat, axis=0, keepdims=True)
    send2[:, 0, :] = flat
    send2[:, 1, :] = jnp.broadcast_to(norm, (slices, LANES))

    my_slot = slot_of(dp, t)
    my_slice = slice_of(dp, t)

    def grads_copy(i):
        d, x = peer(i)
        return pltpu.make_async_remote_copy(
            send2.at[slice_of(d, x)],
            recv2.at[my_slot],
            send2_sem,
            recv2_sem,
            device_id=(d, x),
            device_id_type=MESH,
        )

    each(ndev - 1, lambda i: grads_copy(i).start())
    recv2[my_slot] = send2[my_slice]
    own_query.wait()
    others = queries.at[pl.ds(0, ndp - 1)]
    pltpu.make_async_copy(others, others, query_recv).wait()
    query_terms = right_terms(queries[...].reshape(nq, LANES), 1)
    others = recv2.at[pl.ds(0, ndev - 1)]
    pltpu.make_async_copy(others, others, recv2_sem).wait()

    everyone = recv2[...]
    examples = ndp * nt
    moment = jnp.sum(everyone * everyone, axis=0)[0:1] / examples
    norms = jnp.sum(everyone, axis=0)[1:2]
    mean = jnp.sum(norms, axis=1, keepdims=True) / (examples * rank * rank)
    precond = 1.0 / (moment + DAMPING * mean)
    first = pl.multiple_of(lax.div(dp, group) * slices, slices)
    grads = recv2[pl.ds(first, slices), 0, :]
    scores = contract_last(left_terms(grads * precond, 1), query_terms)
    block = slices // pack
    packed = jnp.concatenate([scores[r * block : (r + 1) * block] for r in range(pack)], axis=1)
    for d in range(group):
        send3[d] = packed[d * per_row : (d + 1) * per_row]

    my_group = lax.div(dp, group)

    def scores_copy(i):
        p = lax.rem(my_slice + i, slices)
        d, x = lax.div(p, nt), lax.rem(p, nt)
        return pltpu.make_async_remote_copy(
            send3.at[d],
            recv3.at[my_slice],
            send3_sem,
            recv3_sem,
            device_id=(my_group * group + d, x),
            device_id_type=MESH,
        )

    each(slices - 1, lambda i: scores_copy(i).start())
    recv3[my_slice] = send3[within(dp)]
    others = recv3.at[pl.ds(0, slices - 1)]
    pltpu.make_async_copy(others, others, recv3_sem).wait()
    total = jnp.sum(recv3[...], axis=0) * (1.0 / rank)
    for r in range(per_row):
        for c in range(pack):
            row = r * pack + c
            out_ref[row : row + 1, :] = total[r : r + 1, c * nq : (c + 1) * nq]

    for s in range(nt - 1):
        reduce_copy(s).wait_send()
    others = queries.at[pl.ds(0, ndp - 1)]
    pltpu.make_async_copy(others, others, query_send).wait()
    others = recv2.at[pl.ds(0, ndev - 1)]
    pltpu.make_async_copy(others, others, send2_sem).wait()
    others = recv3.at[pl.ds(0, slices - 1)]
    pltpu.make_async_copy(others, others, send3_sem).wait()


def per_device(
    ndp, nt, gate_pre, up_pre, out_grad, lengths, proj_hidden, proj_out, query_grads
):
    e_dev, seq, ff = gate_pre.shape
    feats = out_grad.shape[2]
    rank = proj_hidden.shape[1]
    q_dev = query_grads.shape[0]
    nq = q_dev * ndp
    slices = rank * rank // LANES
    group = slices // nt
    assert e_dev == nt and slices % nt == 0 and ndp % group == 0
    pack = max(1, LANES // nq)
    per_row = nt // pack
    halves = 2
    f32, bf16 = jnp.float32, jnp.bfloat16
    dma = pltpu.SemaphoreType.DMA
    in_hbm = pl.BlockSpec(memory_space=pl.ANY)
    return pl.pallas_call(
        functools.partial(kernel, ndp, nt),
        out_shape=jax.ShapeDtypeStruct((e_dev, nq), f32),
        in_specs=[in_hbm] * 7,
        out_specs=pl.BlockSpec(memory_space=pltpu.VMEM),
        scratch_shapes=[
            pltpu.SMEM((e_dev,), jnp.int32),
            pltpu.VMEM((e_dev, seq, ff), bf16),
            pltpu.VMEM((e_dev, seq, ff), bf16),
            pltpu.VMEM((e_dev, seq, feats), bf16),
            pltpu.VMEM((rank, ff), bf16),
            pltpu.VMEM((rank, feats), bf16),
            pltpu.VMEM((ndp, q_dev, LANES), f32),
            pltpu.VMEM((nt - 1, seq, 2 * rank), f32),
            pltpu.VMEM((nt - 1, seq, 2 * rank), f32),
            pltpu.VMEM((rank, rank), f32),
            pltpu.VMEM((slices, 2, LANES), f32),
            pltpu.VMEM((ndp * nt, 2, LANES), f32),
            pltpu.VMEM((group, per_row, pack * nq), f32),
            pltpu.VMEM((slices, per_row, pack * nq), f32),
            dma,
            dma((e_dev, halves)),
            dma((e_dev, halves)),
            dma((e_dev,)),
            dma((halves,)),
            dma,
            dma,
            dma,
            dma,
            dma((nt - 1,)),
            dma((nt - 1,)),
            dma,
            dma,
            dma,
            dma,
        ],
        compiler_params=pltpu.CompilerParams(
            collective_id=0, has_side_effects=True, vmem_limit_bytes=64 * 1024 * 1024
        ),
        cost_estimate=pl.CostEstimate(
            flops=2 * e_dev * seq * (ff + feats) * rank,
            bytes_accessed=4 * e_dev * seq * ff + 2 * e_dev * seq * feats,
            transcendentals=e_dev * seq * ff,
        ),
    )(lengths, gate_pre, up_pre, out_grad, proj_hidden.T, proj_out.T, query_grads)


def solution(mesh):
    in_specs = (
        P("dp", None, "tensor"),
        P("dp", None, "tensor"),
        P("dp", None, "tensor"),
        P("dp"),
        P("tensor", None),
        P("tensor", None),
        P("dp", None),
    )
    return jax.shard_map(
        functools.partial(per_device, mesh.shape["dp"], mesh.shape["tensor"]),
        mesh=mesh,
        in_specs=in_specs,
        out_specs=P("dp", None),
        check_vma=False,
    )
```
